32 devices in a mesh: hist: 4 (over z), rows: 8 (over y, x, core).
Axes of the slice: x: 2, y: 2, z: 4, core: 2. Of those that a mesh axis runs over, the one named last changes fastest.
Arguments:
- g_hist: bfloat16 [88, 64, 88, 128], P('hist', None, 'rows'), may hold values from -0.078125 to 0.078125
- g_last: float32 [64, 88, 128], P(None, 'rows'), may hold values from -6 to 6
- integral_last: float32 [64, 88, 128], P(None, 'rows'), may hold values from -6 to 6
- coupling: float32 [64, 64], replicated, may hold values from 0.5 to 2
- step_re: float32 [64, 64], replicated, may hold values from -1 to 2
- step_im: float32 [64, 64], replicated, may hold values from -0.375 to 0.375
Outputs:
- new_row: float32 [64, 88, 128], P('hist', 'rows')
- new_integral: float32 [64, 88, 128], P('hist', 'rows')
The draws below stay inside these ranges and needn't reach their ends.
All inputs are finite; a program needn't handle non-finite values.
Results may differ from the reference program's by a relative error of at most 0.0055.
Values may be sent and summed in bfloat16 or wider, within the bound.
A program may use at most 64 MiB of HBM per device.

```python
import math
import jax
import jax.numpy as jnp
from jax import lax

NORB = 64
ITERS = 3
NT = 88
H_DEV = 22
N_HIST = 4


def draw_g_last(key, part):
    shape = (NORB, NT, 2 * NORB)
    envelope = (0.5 + jnp.arange(NT, dtype=jnp.float32) / NT)[None, :, None]
    first_key = jax.random.fold_in(jax.random.fold_in(key, 11), 0)
    values = 0.7 * jax.random.normal(first_key, shape, jnp.float32) * envelope
    return jnp.clip(values, -6.0, 6.0)


def draw_step_re(key, part):
    shape = (NORB, NORB)
    first_key = jax.random.fold_in(key, 23)
    noise = jax.random.normal(first_key, shape, jnp.float32)
    values = jnp.eye(NORB, dtype=jnp.float32) + 0.5 * noise / NORB ** 0.5
    return jnp.clip(values, -1.0, 2.0)


def steps_of(own_key, dims, pieces, least, largest):
    def one(position, blocks):
        heights = jax.random.uniform(jax.random.fold_in(jax.random.fold_in(own_key, 6), position), (blocks,), jnp.float32, least / len(pieces), largest / len(pieces))
        return jnp.repeat(jnp.exp(heights), dims[position] // blocks).reshape((-1,) + (1,) * (len(dims) - position - 1))

    loudness = one(*pieces[0])
    for cut in pieces[1:]:
        loudness = loudness * one(*cut)
    return loudness


def bell_draw(own_key, shape, scale, reach, cuts=(), kind=jnp.bfloat16):
    gain = steps_of(own_key, shape, cuts, -0.22, 0.18) if cuts else 1.0
    result = jax.random.normal(own_key, shape, jnp.float32) * scale * gain
    return jnp.minimum(jnp.maximum(result, -reach), reach).astype(kind)


def setup_inputs(seed: int = 0) -> dict:
    streams_of = jax.random.split(jax.random.key(seed), 7)
    return {
        "g_hist": bell_draw(streams_of[0], (NT, NORB, NT, 2 * NORB), (NT * NORB) ** -0.5, 0.078125, ((0, 4), (2, 8))),
        "g_last": draw_g_last(jax.random.fold_in(streams_of[6], 71), 0),
        "integral_last": bell_draw(streams_of[2], (NORB, NT, 2 * NORB), 1.0, 6.0, ((1, 8),), jnp.float32),
        "coupling": jnp.clip(jnp.exp(jax.random.uniform(streams_of[3], (NORB, NORB), jnp.float32, math.log(0.5), math.log(2.0))), 0.5, 2.0),
        "step_re": draw_step_re(jax.random.fold_in(streams_of[6], 71), 0),
        "step_im": bell_draw(streams_of[5], (NORB, NORB), (4 * NORB) ** -0.5, 0.375, (), jnp.float32),
    }


step_size = 0.5
half_step = 0.25


def combine(first, second, width):
    return jnp.concatenate([first[..., :width] - second[..., width:], first[..., width:] + second[..., :width]], -1)


def apply_step(step_re, step_im, field):
    orbits, times, wide = field.shape
    flat = field.reshape(orbits, times * wide)
    first = jnp.dot(step_re, flat, precision=lax.Precision.HIGHEST, preferred_element_type=jnp.float32).reshape(orbits, times, wide)
    second = jnp.dot(step_im, flat, precision=lax.Precision.HIGHEST, preferred_element_type=jnp.float32).reshape(orbits, times, wide)
    return combine(first, second, orbits)


def density(field):
    orbits = field.shape[0]
    mask = jnp.eye(orbits, dtype=jnp.float32)[:, None, :]
    real_part = field[..., :orbits]
    imag_part = field[..., orbits:]
    return jnp.sum((real_part * real_part + imag_part * imag_part) * mask)


def sigma_of(field, coupling, scale, weights):
    orbits = field.shape[0]
    real_part = field[..., :orbits]
    imag_part = field[..., orbits:]
    factor = coupling[:, None, :] * (real_part * real_part + imag_part * imag_part) / scale * weights[None, :, None]
    return jnp.concatenate([factor * real_part, factor * imag_part], -1).astype(jnp.bfloat16)


def contract(sigma, g_hist):
    real_rows = sigma[..., :NORB].reshape(NORB, NT * NORB)
    imag_rows = sigma[..., NORB:].reshape(NORB, NT * NORB)
    left_side = jnp.concatenate([real_rows, imag_rows], 0)
    lefts = left_side.reshape(2 * NORB, N_HIST, H_DEV * NORB).transpose(1, 0, 2)
    blocks = g_hist.reshape(N_HIST, H_DEV * NORB, NT * 2 * NORB)

    def accumulate(carry, pair):
        return carry + jnp.dot(pair[0].astype(jnp.float32), pair[1].astype(jnp.float32), preferred_element_type=jnp.float32), None

    total, unused = lax.scan(accumulate, jnp.zeros((2 * NORB, NT * 2 * NORB), jnp.float32), (lefts, blocks))
    product = total.reshape(2 * NORB, NT, 2 * NORB)
    return combine(product[:NORB], product[NORB:], NORB)


def reference(g_hist, g_last, integral_last, coupling, step_re, step_im):
    weights = step_size * jnp.where(jnp.arange(NT) == 0, 0.5, 1.0).astype(jnp.float32)
    shifted = jnp.concatenate([g_last[..., :NORB] + half_step * integral_last[..., NORB:], g_last[..., NORB:] - half_step * integral_last[..., :NORB]], -1)
    base = apply_step(step_re, step_im, shifted)
    field = g_last
    integral = integral_last
    for iteration in range(ITERS):
        scale = 1.0 + density(field) / (NT * NORB)
        sigma = sigma_of(field, coupling, scale, weights)
        integral = contract(sigma, g_hist)
        field = base + jnp.concatenate([half_step * integral[..., NORB:], -half_step * integral[..., :NORB]], -1)
    return field, integral
```

```python
import functools

import jax
import jax.numpy as jnp
from jax import lax
from jax.experimental import pallas as pl
from jax.experimental.pallas import tpu as pltpu
from jax.sharding import PartitionSpec as P

ITERS = 3
GROUP = 4
HALF = 0.25
STEP = 0.5
MESH = pl.DeviceIdType.MESH


def kernel(
    hist, rows, count, orbits, share, tall,
    g_ref, gl_ref, il_ref, coup_ref, re_ref, im_ref,
    row_ref, int_ref,
    ghist, ebuf, lbuf, dbuf, base, tbuf, tsend, trecv, dacc, pcol, prow, inv_ref,
    gsem, esend, lrecv, osend, orecv, ssend, srecv, csend, crecv, wsend, wrecv,
):
    wide = 2 * orbits
    groups = -(-count // GROUP)
    chips = rows // 2
    cells = float(count * rows * orbits)
    mark_at = 4 * tall
    h = lax.axis_index("hist")
    r = lax.axis_index("rows")
    q = r // 2
    k = r % 2
    other = 1 - k
    partner = r + 1 - 2 * k
    home = h == q
    away = jnp.logical_not(home)
    mine = pl.ds(pl.multiple_of(h * share, share), tall)

    loading = pltpu.make_async_copy(g_ref, ghist, gsem)
    loading.start()

    def sizes(g):
        return min(GROUP, count - g * GROUP)

    def loop(low, high, body):
        def step(o, c):
            body(o)
            return c

        lax.fori_loop(low, high, step, 0)

    barrier = pltpu.get_barrier_semaphore()

    def greet(hh, rr):
        pl.semaphore_signal(barrier, inc=1, device_id=(hh, rr), device_id_type=MESH)

    loop(1, hist, lambda o: greet((h + o) % hist, r))
    loop(1, rows, lambda o: greet(h, (r + o) % rows))

    @pl.when(away)
    def _():
        loop(1, hist, lambda o: greet((h + o) % hist, 2 * h + k))

    near = hist - 1 + rows - 1
    lane = lax.broadcasted_iota(jnp.int32, (tall, wide), 1)
    line = lax.broadcasted_iota(jnp.int32, (tall, wide), 0)
    low = lane < orbits
    minus_plus = jnp.where(low, -1.0, 1.0).astype(jnp.float32)
    here = line + h * share
    diagonal = (line < share) & ((lane == here) | (lane == here + orbits))
    eye = jnp.where(diagonal, 1.0, 0.0).astype(jnp.float32)
    coup_rows = coup_ref[mine, :]
    coup = jnp.concatenate([coup_rows, coup_rows], 1)

    def turn(x):
        return pltpu.roll(x, orbits, 1)

    def joined(first, second):
        return first + minus_plus * turn(second)

    def sigma_copy(it, g, o):
        target = (q + o) % chips
        return pltpu.make_async_remote_copy(
            src_ref=ebuf.at[it, g],
            dst_ref=lbuf.at[it, k, g, h],
            send_sem=esend.at[it, g, o],
            recv_sem=lrecv.at[it, g, h],
            device_id=(q, 2 * target + k),
            device_id_type=MESH,
        )

    def sigma_from(it, g, source):
        return pltpu.make_async_remote_copy(
            src_ref=ebuf.at[it, g],
            dst_ref=lbuf.at[it, k, g, source],
            send_sem=esend.at[it, g, 0],
            recv_sem=lrecv.at[it, g, source],
            device_id=(source, 2 * h + k),
            device_id_type=MESH,
        )

    def pair_copy(it, g, member):
        return pltpu.make_async_remote_copy(
            src_ref=lbuf.at[it, member, g],
            dst_ref=lbuf.at[it, member, g],
            send_sem=osend.at[it, g],
            recv_sem=orecv.at[it, g],
            device_id=(h, partner),
            device_id_type=MESH,
        )

    def column_copy(it, o):
        return pltpu.make_async_remote_copy(
            src_ref=pcol.at[it, h],
            dst_ref=pcol.at[it, h],
            send_sem=csend.at[it, o],
            recv_sem=crecv.at[it, h],
            device_id=((h + o) % hist, r),
            device_id_type=MESH,
        )

    def column_from(it, source):
        return pltpu.make_async_remote_copy(
            src_ref=pcol.at[it, source],
            dst_ref=pcol.at[it, source],
            send_sem=csend.at[it, 0],
            recv_sem=crecv.at[it, source],
            device_id=(source, r),
            device_id_type=MESH,
        )

    def plane_copy(it, o):
        return pltpu.make_async_remote_copy(
            src_ref=prow.at[it, r],
            dst_ref=prow.at[it, r],
            send_sem=wsend.at[it, o],
            recv_sem=wrecv.at[it, r],
            device_id=(h, (r + o) % rows),
            device_id_type=MESH,
        )

    def plane_from(it, source):
        return pltpu.make_async_remote_copy(
            src_ref=prow.at[it, source],
            dst_ref=prow.at[it, source],
            send_sem=wsend.at[it, 0],
            recv_sem=wrecv.at[it, source],
            device_id=(h, source),
            device_id_type=MESH,
        )

    def terms_copy(it, g, target, source):
        times = pl.ds(g * GROUP, sizes(g))
        return pltpu.make_async_remote_copy(
            src_ref=tsend.at[it, target, times],
            dst_ref=trecv.at[it, source, times],
            send_sem=ssend.at[it, g, target],
            recv_sem=srecv.at[it, g, source],
            device_id=(target, r),
            device_id_type=MESH,
        )

    def make_sigma(it, g, fields):
        norms = []
        total = jnp.zeros((tall, wide), jnp.float32)
        for f in fields:
            sq = f * f
            n2 = sq + turn(sq)
            norms.append(n2)
            total = total + n2 * (1.0 / (GROUP * tall * wide))
        mean = 1.0 + jnp.sum(total, keepdims=True)
        mark = jnp.broadcast_to(mean, (16, wide)).astype(jnp.bfloat16)
        inverse = 1.0 / mark.astype(jnp.float32)[0:1, :]
        taus = []
        for i, f in enumerate(fields):
            weight = STEP
            if g == 0 and i == 0:
                weight = jnp.where(r == 0, 0.5 * STEP, STEP).astype(jnp.float32)
            taus.append(norms[i] * (inverse * weight) * coup * f)
        while len(taus) < GROUP:
            taus.append(jnp.zeros((tall, wide), jnp.float32))
        parts = []
        for p in range(GROUP // 2):
            a, b = taus[2 * p], taus[2 * p + 1]
            parts.append(jnp.where(low, a, turn(b)).astype(jnp.bfloat16))
            parts.append(jnp.where(low, turn(a), b).astype(jnp.bfloat16))
        for i, part in enumerate(parts):
            ebuf[it, g, pl.ds(i * tall, tall), :] = part
        ebuf[it, g, pl.ds(mark_at, 16), :] = mark

        @pl.when(home)
        def _():
            for i, part in enumerate(parts):
                lbuf[it, k, g, h, pl.ds(i * tall, tall), :] = part
            lbuf[it, k, g, h, pl.ds(mark_at, 16), :] = mark

    def send_sigma(it, g):
        loop(1, chips, lambda o: sigma_copy(it, g, o).start())

        @pl.when(away)
        def _():
            sigma_copy(it, g, 0).start()

    def send_power(it):
        pcol[it, h] = jnp.broadcast_to(jnp.sum(dacc[...], keepdims=True), (8, wide))
        loop(1, hist, lambda o: column_copy(it, o).start())

    def pass_power(it):
        loop(1, hist, lambda o: column_from(it, (h + o) % hist).wait_recv())
        prow[it, r] = jnp.sum(pcol[it], axis=0)
        loop(1, rows, lambda o: plane_copy(it, o).start())

    def take_scale(it):
        loop(1, rows, lambda o: plane_from(it, (r + o) % rows).wait_recv())
        inv_ref[...] = 1.0 / (1.0 + jnp.sum(prow[it], axis=0) * (1.0 / cells))

    dacc[...] = jnp.zeros((tall, wide), jnp.float32)
    for g in range(groups):
        fields = [gl_ref[g * GROUP + i, mine, :] for i in range(sizes(g))]
        for f in fields:
            dacc[...] += f * f * eye
        make_sigma(0, g, fields)

    @pl.when(away)
    def _():
        pl.semaphore_wait(barrier, near + chips - 1)

    @pl.when(home)
    def _():
        pl.semaphore_wait(barrier, near)

    for g in range(groups):
        send_sigma(0, g)
    send_power(0)

    step = jnp.concatenate([re_ref[mine, :], im_ref[mine, :]], 0)
    whole_sign = jnp.where(
        lax.broadcasted_iota(jnp.int32, (orbits, wide), 1) < orbits, HALF, -HALF
    ).astype(jnp.float32)
    for t in range(count):
        shifted = gl_ref[t, pl.ds(0, orbits), :] + whole_sign * turn(il_ref[t])
        both = jnp.dot(
            step, shifted, precision=lax.Precision.HIGHEST,
            preferred_element_type=jnp.float32,
        )
        base[t] = joined(both[:tall], both[tall:])

    def multiply_pair(it, member, j, place, t):
        left = jnp.concatenate(
            [
                jnp.concatenate(
                    [
                        lbuf[it, member, j, s, pl.ds(2 * p * tall, 2 * tall), :]
                        for s in range(hist)
                    ],
                    0,
                )
                for p in range(GROUP // 2)
            ],
            1,
        )[:, :sizes(j) * orbits]
        first = member * count + j * GROUP
        pair = range(t, min(t + 2, count))
        right = jnp.concatenate(
            [
                jnp.concatenate([ghist[first + i, u] for i in range(sizes(j))], 0)
                for u in pair
            ],
            1,
        )
        dbuf[place, j, :, t * wide:(t + len(pair)) * wide] = jnp.dot(
            left, right, preferred_element_type=jnp.float32
        )

    def multiply(it, member, j, place):
        for t in range(0, count, 2):
            multiply_pair(it, member, j, place, t)

    def iteration(it, c):
        pass_power(it)
        for j in range(groups):
            @pl.when(away)
            def _():
                sigma_from(it, j, h).wait_recv()

            loop(1, hist, lambda o: sigma_from(it, j, (h + o) % hist).wait_recv())
            pair_copy(it, j, k).start()

            if j == 0:
                @pl.when(it == 0)
                def _():
                    loading.wait()
            if j > 0:
                pair_copy(it, j - 1, other).wait_recv()
                multiply(it, other, j - 1, 1)
            multiply(it, k, j, 0)
        take_scale(it)
        pair_copy(it, groups - 1, other).wait_recv()

        inv = inv_ref[0:1, :]
        facs = []
        for s in range(hist):
            for place, member in ((0, k), (1, other)):
                for j in range(groups):
                    mark = lbuf[it, member, j, s, pl.ds(mark_at, 16), :].astype(jnp.float32)
                    facs.append((s, place, j, mark[0:1, :] * inv))
        for g in range(groups):
            for t in range(g * GROUP, g * GROUP + sizes(g)):
                if t % 2 == 0:
                    multiply_pair(it, other, groups - 1, 1, t)
                for s in range(hist):
                    product = None
                    for at, place, j, fac in facs:
                        if at == s:
                            piece = dbuf[
                                place, j, 2 * tall * s:2 * tall * (s + 1),
                                t * wide:(t + 1) * wide,
                            ] * fac
                            product = piece if product is None else product + piece
                    value = joined(product[:tall], product[tall:])
                    tbuf[s, t] = value
                    tsend[it, s, t] = value.astype(jnp.bfloat16)
            loop(1, hist, lambda o: terms_copy(it, g, (h + o) % hist, h).start())

        dacc[...] = jnp.zeros((tall, wide), jnp.float32)
        for g in range(groups):
            span = range(g * GROUP, g * GROUP + sizes(g))

            def add(o):
                source = (h + o) % hist
                terms_copy(it, g, source, source).wait_recv()
                for t in span:
                    tbuf[h, t] += trecv[it, source, t].astype(jnp.float32)

            loop(1, hist, add)
            fields = []
            for t in span:
                total = tbuf[h, t]
                f = base[t] - (HALF * minus_plus) * turn(total)
                dacc[...] += f * f * eye
                fields.append(f)

            @pl.when(it == ITERS - 1)
            def _():
                for i, t in enumerate(span):
                    int_ref[t] = tbuf[h, t][:share]
                    row_ref[t] = fields[i][:share]

            @pl.when(it < ITERS - 1)
            def _():
                make_sigma(it + 1, g, fields)
                send_sigma(it + 1, g)
                if g == groups - 1:
                    send_power(it + 1)

        for g in range(groups):
            loop(1, chips, lambda o: sigma_copy(it, g, o).wait_send())

            @pl.when(away)
            def _():
                sigma_copy(it, g, 0).wait_send()

            pair_copy(it, g, k).wait_send()
            loop(1, hist, lambda o: terms_copy(it, g, (h + o) % hist, h).wait_send())
        loop(1, hist, lambda o: column_copy(it, o).wait_send())
        loop(1, rows, lambda o: plane_copy(it, o).wait_send())
        return c

    lax.fori_loop(0, ITERS, iteration, 0)


def on_device(g_hist, g_last, integral_last, coupling, step_re, step_im):
    orbits, count, wide = g_last.shape
    hist = lax.axis_size("hist")
    rows = lax.axis_size("rows")
    assert rows == 2 * hist and g_hist.shape[0] == 2 * count
    groups = -(-count // GROUP)
    share = orbits // hist
    tall = -(-share // 16) * 16
    columns = count * wide
    history_shape = (g_hist.shape[0], count, orbits, wide)
    history = g_hist.transpose(0, 2, 1, 3)
    field = g_last.transpose(1, 0, 2)
    before = integral_last.transpose(1, 0, 2)
    if tall > share:
        extra = tall - share
        field = jnp.pad(field, ((0, 0), (0, extra), (0, 0)))
        coupling = jnp.pad(coupling, ((0, extra), (0, 0)))
        step_re = jnp.pad(step_re, ((0, extra), (0, 0)))
        step_im = jnp.pad(step_im, ((0, extra), (0, 0)))
    dma = pltpu.SemaphoreType.DMA
    part = jax.ShapeDtypeStruct((count, share, wide), jnp.float32)
    chunk = 4 * tall + 16
    row, integral = pl.pallas_call(
        functools.partial(kernel, hist, rows, count, orbits, share, tall),
        out_shape=(part, part),
        in_specs=[pl.BlockSpec(memory_space=pl.ANY)]
        + [pl.BlockSpec(memory_space=pltpu.VMEM)] * 5,
        out_specs=(pl.BlockSpec(memory_space=pltpu.VMEM),) * 2,
        scratch_shapes=[
            pltpu.VMEM(history_shape, jnp.bfloat16),
            pltpu.VMEM((ITERS, groups, chunk, wide), jnp.bfloat16),
            pltpu.VMEM((ITERS, 2, groups, hist, chunk, wide), jnp.bfloat16),
            pltpu.VMEM((2, groups, 2 * tall * hist, columns), jnp.float32),
            pltpu.VMEM((count, tall, wide), jnp.float32),
            pltpu.VMEM((hist, count, tall, wide), jnp.float32),
            pltpu.VMEM((ITERS, hist, count, tall, wide), jnp.bfloat16),
            pltpu.VMEM((ITERS, hist, count, tall, wide), jnp.bfloat16),
            pltpu.VMEM((tall, wide), jnp.float32),
            pltpu.VMEM((ITERS, hist, 8, wide), jnp.float32),
            pltpu.VMEM((ITERS, rows, 8, wide), jnp.float32),
            pltpu.VMEM((8, wide), jnp.float32),
            dma,
            dma((ITERS, groups, rows // 2)),
            dma((ITERS, groups, hist)),
            dma((ITERS, groups)),
            dma((ITERS, groups)),
            dma((ITERS, groups, hist)),
            dma((ITERS, groups, hist)),
            dma((ITERS, hist)),
            dma((ITERS, hist)),
            dma((ITERS, rows)),
            dma((ITERS, rows)),
        ],
        compiler_params=pltpu.CompilerParams(
            collective_id=0, has_side_effects=True, vmem_limit_bytes=60 * 1024 * 1024
        ),
        cost_estimate=pl.CostEstimate(
            flops=ITERS * 4 * wide * count * orbits * columns,
            bytes_accessed=4 * count * orbits * columns,
            transcendentals=0,
        ),
        name="memory_steps",
    )(history, field, before, coupling, step_re, step_im)
    return (row.transpose(1, 0, 2), integral.transpose(1, 0, 2))


def solution(mesh):
    in_specs = (
        P("hist", None, "rows", None),
        P(None, "rows", None),
        P(None, "rows", None),
        P(),
        P(),
        P(),
    )
    out_specs = (P("hist", "rows", None), P("hist", "rows", None))
    return jax.shard_map(
        on_device, mesh=mesh, in_specs=in_specs, out_specs=out_specs, check_vma=False
    )
```
